32 devices in a mesh: zone: 8 (over z, y), var: 4 (over x, core).
Axes of the slice: x: 2, y: 2, z: 4, core: 2. Of those that a mesh axis runs over, the one named last changes fastest.
Arguments:
- history: float32 [48, 64, 4096], P('var', None, 'zone'), may hold values from -6 to 6
- adjacency: int32 [6, 4096], P(None, 'zone'), may hold values from -1 to 4095, as said below
- volume_op: float32 [64, 64], replicated, may hold values from -0.375 to 0.375
- face_lift: float32 [6, 64, 64], replicated, may hold values from -0.1875 to 0.1875
- schmid_map: float32 [48, 12], replicated, may hold values from -0.875 to 0.875
- hardening: float32 [12, 48], replicated, may hold values from -1.75 to 1.75
Outputs:
- remapped: float32 [48, 64, 4096], P('var', None, 'zone')
The draws below stay inside these ranges and needn't reach their ends.
Inputs may be any that keep to these rules, and one draw needn't show every extreme that they name: `adjacency`: every entry is -1 or a zone whose index differs from the zone's own by at most 64; differences of exactly 64 and -64 occur.
All inputs are finite; a program needn't handle non-finite values.
Results may differ from the reference program's by a relative error of at most 0.0001.
Values sent between devices are 32-bit elements; how exact they have to be, the bound alone decides.
A program may use at most 128 MiB of HBM per device.

```python
import jax
import jax.numpy as jnp
from jax import lax

V = 48
P_SIZE = 64
SLIP = 12
ZDEV = 512
ZONES = 4096
RIM = 64
N_VAR = 4


def draw_adjacency(key, part):
    zone_ids = jnp.arange(ZONES, dtype=jnp.int32)
    position = zone_ids % ZDEV
    offsets = jax.random.randint(jax.random.fold_in(key, 11), (6, ZONES), -RIM, RIM + 1)
    offsets = offsets.at[0].set(jnp.where(position == ZDEV - 1, RIM, offsets[0]))
    offsets = offsets.at[1].set(jnp.where(position == 0, -RIM, offsets[1]))
    offsets = offsets.at[2].set(jnp.where(position == ZDEV - 2, 1, offsets[2]))
    target = zone_ids[None, :] + offsets
    open_face = jax.random.randint(jax.random.fold_in(key, 12), (6, ZONES), 0, 16)
    keep_face = (open_face != 0) | (jnp.arange(6)[:, None] < 3)
    target = jnp.where((target < 0) | (target >= ZONES) | jnp.logical_not(keep_face), -1, target)
    return target.astype(jnp.int32)


def block_scale(rng, dims, cuts, smallest, high):
    def one(dim, parts):
        draws = jax.random.uniform(jax.random.fold_in(jax.random.fold_in(rng, 6), dim), (parts,), jnp.float32, smallest / len(cuts), high / len(cuts))
        return jnp.repeat(jnp.exp(draws), dims[dim] // parts).reshape((-1,) + (1,) * (len(dims) - dim - 1))

    level = one(*cuts[0])
    for cut in cuts[1:]:
        level = level * one(*cut)
    return level


def noise(rng, dims, deviation, bound, split=(), kind=jnp.bfloat16):
    array = deviation * jax.random.normal(rng, dims, jnp.float32)
    if split:
        array = array * block_scale(rng, dims, split, -0.22, 0.18)
    return jnp.clip(array, -bound, bound).astype(kind)


def setup_inputs(seed: int = 0) -> dict:
    splits = jax.random.split(jax.random.key(seed), 7)
    history = noise(splits[0], (V, P_SIZE, ZONES), 1.0, 6.0, ((0, 4), (2, 8)), jnp.float32)
    adjacency = draw_adjacency(jax.random.fold_in(splits[6], 71), 0)
    volume_op = noise(splits[2], (P_SIZE, P_SIZE), (4 * P_SIZE) ** -0.5, 0.375, (), jnp.float32)
    face_lift = noise(splits[3], (6, P_SIZE, P_SIZE), (16 * P_SIZE) ** -0.5, 0.1875, (), jnp.float32)
    schmid_map = noise(splits[4], (V, SLIP), V ** -0.5, 0.875, (), jnp.float32)
    hardening = noise(splits[5], (SLIP, V), SLIP ** -0.5, 1.75, (), jnp.float32)
    return {"history": history, "adjacency": adjacency, "volume_op": volume_op, "face_lift": face_lift, "schmid_map": schmid_map, "hardening": hardening}


def advect_operator(field, adjacency, volume_op, face_lift):
    result = jnp.dot(volume_op.T, field, precision=lax.Precision.HIGHEST)
    for face in range(6):
        face_index = adjacency[face]
        safe_index = jnp.clip(face_index, 0, ZONES - 1).astype(jnp.int32)
        neighbour = jnp.take(field, safe_index, axis=1)
        neighbour = jnp.where(face_index[None, :] >= 0, neighbour, jnp.float32(0.0))
        result = result + jnp.dot(face_lift[face].T, neighbour, precision=lax.Precision.HIGHEST)
    return result

def advect_variable(field, adjacency, volume_op, face_lift):
    section_one = field + advect_operator(field, adjacency, volume_op, face_lift)
    section_two = 0.75 * field + 0.25 * (section_one + advect_operator(section_one, adjacency, volume_op, face_lift))
    return field / 3.0 + 2.0 / 3.0 * (section_two + advect_operator(section_two, adjacency, volume_op, face_lift))

def reference(history, adjacency, volume_op, face_lift, schmid_map, hardening):
    advected = lax.map(lambda field: advect_variable(field, adjacency, volume_op, face_lift), history)
    shear = jnp.einsum('va,vpz->apz', schmid_map, advected, precision=lax.Precision.HIGHEST)
    updated = advected + jnp.einsum('av,apz->vpz', hardening, jnp.tanh(shear), precision=lax.Precision.HIGHEST)
    stride = V // N_VAR
    rotation = updated[0:4 * stride:stride]
    length = jnp.sqrt(lax.optimization_barrier(jnp.sum(rotation * rotation, axis=0)))
    factor = 1.0 / jnp.maximum(length, 1.0)
    return updated.at[0:4 * stride:stride].multiply(factor[None])
```

```python
import functools

import jax
import jax.numpy as jnp
from jax import lax
from jax.experimental import pallas as pl
from jax.experimental.pallas import tpu as pltpu
from jax.sharding import PartitionSpec as P

F32 = jnp.float32
BF16 = jnp.bfloat16
MESH = pl.DeviceIdType.MESH
ROT = 4
TILE = 16


def split(x):
    hi = x.astype(BF16)
    return hi, (x - hi.astype(F32)).astype(BF16)


def kernel(sizes, adj_ref, op_ref, schmid_ref, hard_ref, h_ref, out_ref, cur, acc, lcat, wown, wmer,
           ohown, ohmer, hsend, hrecv, msg, mrecv, buf, tb,
           hs_sem, hr_sem, m_sem, mr_sem, x_sem, xr_sem, t_sem, tr_sem):
    zones_n, chips_n, vl, pts, local, faces, slips = sizes
    rim = local // 8
    lane = 2 * rim
    blk = 2 * lane
    half = vl * pts // 2
    zone = lax.axis_index("zone")
    var = lax.axis_index("var")
    chip = var // 2
    core = var % 2
    mate = chip * 2 + (1 - core)
    has_left = zone > 0
    has_right = zone < zones_n - 1
    low = lax.broadcasted_iota(jnp.int32, (pts, lane), 1) < rim

    barrier = pltpu.get_barrier_semaphore()

    @pl.when(has_left)
    def _():
        pl.semaphore_signal(barrier, inc=1, device_id={"zone": zone - 1}, device_id_type=MESH)

    @pl.when(has_right)
    def _():
        pl.semaphore_signal(barrier, inc=1, device_id={"zone": zone + 1}, device_id_type=MESH)

    pl.semaphore_signal(barrier, inc=1, device_id={"var": mate}, device_id_type=MESH)
    for d in range(1, chips_n):
        peer = ((chip + d) % chips_n) * 2 + core
        pl.semaphore_signal(barrier, inc=1, device_id={"var": peer}, device_id_type=MESH)

    def halo_copy(s, side):
        target = zone + 1 if side == 0 else zone - 1
        return pltpu.make_async_remote_copy(
            src_ref=hsend.at[s, side], dst_ref=hrecv.at[s, side],
            send_sem=hs_sem.at[s, side], recv_sem=hr_sem.at[s, side],
            device_id={"zone": target}, device_id_type=MESH)

    def pack_edges(s, src):
        def body(i, _):
            top = pl.ds(pl.multiple_of(i * pts, pts), pts)
            bot = pl.ds(pl.multiple_of(half + i * pts, pts), pts)
            hsend[s, 0, top, :] = jnp.where(
                low, pltpu.roll(src[top, local - lane:local], rim, 1), src[bot, local - lane:local])
            hsend[s, 1, top, :] = jnp.where(
                low, src[top, 0:lane], pltpu.roll(src[bot, 0:lane], rim, 1))
            return 0
        lax.fori_loop(0, vl // 2, body, 0)

    def start_halo(s):
        @pl.when(has_right)
        def _():
            halo_copy(s, 0).start()

        @pl.when(has_left)
        def _():
            halo_copy(s, 1).start()

    def wait_halo(s):
        @pl.when(has_left)
        def _():
            halo_copy(s, 0).wait_recv()

        @pl.when(has_right)
        def _():
            halo_copy(s, 1).wait_recv()

    pack_edges(0, h_ref)

    @pl.when(jnp.logical_not(has_left))
    def _():
        for s in range(3):
            hrecv[s, 0] = jnp.zeros((half, lane), F32)

    @pl.when(jnp.logical_not(has_right))
    def _():
        for s in range(3):
            hrecv[s, 1] = jnp.zeros((half, lane), F32)

    pl.semaphore_wait(barrier, chips_n + has_left.astype(jnp.int32) + has_right.astype(jnp.int32))
    start_halo(0)

    rows_all = (faces + 1) * pts
    op_hi, op_lo = split(op_ref[...])
    first = lax.broadcasted_iota(jnp.int32, (rows_all, 4 * pts), 1) < 2 * pts
    lcat[...] = jnp.where(first, op_hi.astype(F32), op_lo.astype(F32)).astype(BF16)

    offset = zone * local
    k_own = lax.broadcasted_iota(jnp.int32, (blk, blk), 0)
    k_mer = lax.broadcasted_iota(jnp.int32, (lane, blk), 0)
    for b in range(2):
        src_mer = jnp.where(k_mer < rim, blk * (b + 1) + k_mer, blk * b - lane + k_mer)
        for f in range(faces):
            adj = adj_ref[f:f + 1, b * blk:(b + 1) * blk]
            adj = jnp.where(adj >= 0, adj - offset, -4 * local)
            ohown[b, f * blk:(f + 1) * blk, :] = jnp.where(
                k_own + b * blk == adj, 1.0, 0.0).astype(BF16)
            ohmer[b, f * lane:(f + 1) * lane, :] = jnp.where(
                src_mer == adj, 1.0, 0.0).astype(BF16)

    def v_rows(v):
        return pl.ds(pl.multiple_of(v * pts, pts), pts)

    def put(ref, v, col, width, w):
        hi, lo = split(w)
        ref[pl.ds(pl.multiple_of(v * 2 * pts, pts), pts), col:col + width] = hi
        ref[pl.ds(pl.multiple_of(v * 2 * pts + pts, pts), pts), col:col + width] = lo

    def lift_own(src):
        def body(v, _):
            rows = v_rows(v)
            for b in range(2):
                u = src[rows, b * blk:(b + 1) * blk]
                hi, lo = split(u)
                w = jnp.dot(lcat[...], jnp.concatenate([hi, lo, hi, lo], axis=0),
                            preferred_element_type=F32)
                acc[rows, b * blk:(b + 1) * blk] = u + w[faces * pts:]
                for f in range(faces):
                    put(wown, v, (b * faces + f) * blk, blk, w[f * pts:(f + 1) * pts])
            return 0
        lax.fori_loop(0, vl, body, 0)

    def lift_merged(s, src):
        def one(v, left, right):
            rows = v_rows(v)
            m0 = jnp.where(low, src[rows, blk:blk + lane], left)
            m1 = jnp.where(low, right, src[rows, blk - lane:blk])
            hi, lo = split(jnp.concatenate([m0, m1], axis=1))
            w = jnp.dot(lcat[0:faces * pts, :], jnp.concatenate([hi, lo, hi, lo], axis=0),
                        preferred_element_type=F32)
            for b in range(2):
                for f in range(faces):
                    put(wmer, v, (b * faces + f) * lane, lane,
                        w[f * pts:(f + 1) * pts, b * lane:(b + 1) * lane])

        def body(i, _):
            rows = v_rows(i)
            left, right = hrecv[s, 0, rows, :], hrecv[s, 1, rows, :]
            one(i, pltpu.roll(left, rim, 1), right)
            one(i + vl // 2, left, pltpu.roll(right, rim, 1))
            return 0
        lax.fori_loop(0, vl // 2, body, 0)

    group = 4 if vl % 4 == 0 else 3 if vl % 3 == 0 else 1

    def select(lhs, rhs, b, width, finish):
        def body(g, _):
            r = jnp.dot(
                lhs[pl.ds(pl.multiple_of(g * group * 2 * pts, 2 * pts), group * 2 * pts),
                    b * faces * width:(b + 1) * faces * width],
                rhs[b], preferred_element_type=F32)
            for j in range(group):
                part = r[2 * j * pts:(2 * j + 1) * pts] + r[(2 * j + 1) * pts:(2 * j + 2) * pts]
                finish(v_rows(g * group + j), slice(b * blk, (b + 1) * blk), part)
            return 0
        lax.fori_loop(0, vl // group, body, 0)

    def add(rows, cols, part):
        acc[rows, cols] += part

    def finish_for(s):
        def finish(rows, cols, part):
            total = acc[rows, cols] + part
            if s == 0:
                cur[rows, cols] = total
            elif s == 1:
                cur[rows, cols] = 0.75 * h_ref[rows, cols] + 0.25 * total
            else:
                cur[rows, cols] = h_ref[rows, cols] * (1.0 / 3.0) + (2.0 / 3.0) * total
        return finish

    def shear_chunk(col, dest, rot_row):
        def body(t, _):
            tr = pl.ds(pl.multiple_of(t * TILE, TILE), TILE)
            xs = [cur[pl.ds(pl.multiple_of(v * pts + t * TILE, TILE), TILE), pl.ds(col, lane)]
                  for v in range(vl)]
            for a in range(slips):
                y = xs[0] * schmid_ref[var * vl, a]
                for v in range(1, vl):
                    y = y + xs[v] * schmid_ref[var * vl + v, a]
                dest[a, tr, :] = y
            dest[rot_row, tr, :] = xs[0]
            return 0
        lax.fori_loop(0, pts // TILE, body, 0)

    def chunk_col(b, c):
        return pl.multiple_of(b * blk + c * lane, lane)

    def mate_copy(b):
        return pltpu.make_async_remote_copy(
            src_ref=msg.at[b], dst_ref=mrecv.at[b], send_sem=m_sem.at[b], recv_sem=mr_sem.at[b],
            device_id={"var": mate}, device_id_type=MESH)

    def chip_copy(b, d, slot):
        peer = ((chip + d) % chips_n) * 2 + core
        return pltpu.make_async_remote_copy(
            src_ref=buf.at[b, slot], dst_ref=buf.at[b, slot],
            send_sem=x_sem.at[b, d - 1], recv_sem=xr_sem.at[b, slot],
            device_id={"var": peer}, device_id_type=MESH)

    def tanh_copy(b, slot):
        return pltpu.make_async_remote_copy(
            src_ref=tb.at[b, slot], dst_ref=tb.at[b, slot],
            send_sem=t_sem.at[b], recv_sem=tr_sem.at[b],
            device_id={"var": mate}, device_id_type=MESH)

    def send_partial(b):
        shear_chunk(chunk_col(b, 1 - core), msg.at[b], slips)
        mate_copy(b).start()
        shear_chunk(chunk_col(b, core), buf.at[b, chip], slips + core)

    def send_chip(b):
        mate_copy(b).wait_recv()
        mine = buf.at[b, chip]
        for a in range(slips):
            mine[a] = mine[a] + mrecv[b, a]
        mine[slips + 1 - core] = mrecv[b, slips]
        for d in range(1, chips_n):
            chip_copy(b, d, chip).start()

    def renew(b):
        for d in range(1, chips_n):
            chip_copy(b, d, (chip + d) % chips_n).wait_recv()

        def body(t, _):
            tr = pl.ds(pl.multiple_of(t * TILE, TILE), TILE)
            ts = []
            for a in range(slips):
                y = buf[b, 0, a, tr, :]
                for c in range(1, chips_n):
                    y = y + buf[b, c, a, tr, :]
                ts.append(jnp.tanh(y))
                tb[b, core, a, tr, :] = ts[-1]
            total = None
            for k in range(ROT):
                y = buf[b, k // 2, slips + k % 2, tr, :]
                for a in range(slips):
                    y = y + ts[a] * hard_ref[a, k * vl]
                total = y * y if total is None else total + y * y
            tb[b, core, slips, tr, :] = 1.0 / jnp.maximum(jnp.sqrt(total), 1.0)
            return 0
        lax.fori_loop(0, pts // TILE, body, 0)
        tanh_copy(b, core).start()

    rotates = (jnp.full((TILE, lane), var, jnp.int32) < ROT)

    def write(b, c):
        col = chunk_col(b, c)

        def body(t, _):
            tr = pl.ds(pl.multiple_of(t * TILE, TILE), TILE)
            ts = [tb[b, c, a, tr, :] for a in range(slips)]
            for v in range(vl):
                rows = pl.ds(pl.multiple_of(v * pts + t * TILE, TILE), TILE)
                y = cur[rows, pl.ds(col, lane)]
                for a in range(slips):
                    y = y + ts[a] * hard_ref[a, var * vl + v]
                if v == 0:
                    y = jnp.where(rotates, y * tb[b, c, slips, tr, :], y)
                out_ref[rows, pl.ds(col, lane)] = y
            return 0
        lax.fori_loop(0, pts // TILE, body, 0)

    for s in range(3):
        src = h_ref if s == 0 else cur
        lift_own(src)
        for b in range(2):
            select(wown, ohown, b, blk, add)
        wait_halo(s)
        lift_merged(s, src)
        for b in range(2):
            select(wmer, ohmer, b, lane, finish_for(s))
            if s == 2:
                send_partial(b)
        if s < 2:
            pack_edges(s + 1, cur)
            start_halo(s + 1)

    for b in range(2):
        send_chip(b)
    for b in range(2):
        renew(b)
    for b in range(2):
        write(b, core)
    for b in range(2):
        tanh_copy(b, 1 - core).wait_recv()
        write(b, 1 - core)

    for s in range(3):
        @pl.when(has_right)
        def _():
            halo_copy(s, 0).wait_send()

        @pl.when(has_left)
        def _():
            halo_copy(s, 1).wait_send()
    for b in range(2):
        mate_copy(b).wait_send()
        tanh_copy(b, core).wait_send()
        for d in range(1, chips_n):
            chip_copy(b, d, chip).wait_send()


def per_device(zones_n, chips_n, history, adjacency, volume_op, face_lift, schmid_map, hardening):
    vl, pts, local = history.shape
    faces = face_lift.shape[0]
    slips = schmid_map.shape[1]
    lane, blk, half = local // 4, local // 2, vl * pts // 2
    ops = jnp.concatenate([face_lift, volume_op[None]], axis=0)
    ops = jnp.tile(jnp.swapaxes(ops, 1, 2).reshape((faces + 1) * pts, pts), (1, 4))
    vmem = pl.BlockSpec(memory_space=pltpu.VMEM)
    smem = pl.BlockSpec(memory_space=pltpu.SMEM)
    dma = pltpu.SemaphoreType.DMA
    out = pl.pallas_call(
        functools.partial(kernel, (zones_n, chips_n, vl, pts, local, faces, slips)),
        out_shape=jax.ShapeDtypeStruct((vl * pts, local), F32),
        in_specs=[vmem, vmem, smem, smem, vmem],
        out_specs=vmem,
        scratch_shapes=[
            pltpu.VMEM((vl * pts, local), F32),
            pltpu.VMEM((vl * pts, local), F32),
            pltpu.VMEM(((faces + 1) * pts, 4 * pts), BF16),
            pltpu.VMEM((vl * 2 * pts, 2 * faces * blk), BF16),
            pltpu.VMEM((vl * 2 * pts, 2 * faces * lane), BF16),
            pltpu.VMEM((2, faces * blk, blk), BF16),
            pltpu.VMEM((2, faces * lane, blk), BF16),
            pltpu.VMEM((3, 2, half, lane), F32),
            pltpu.VMEM((3, 2, half, lane), F32),
            pltpu.VMEM((2, slips + 1, pts, lane), F32),
            pltpu.VMEM((2, slips + 1, pts, lane), F32),
            pltpu.VMEM((2, chips_n, slips + 2, pts, lane), F32),
            pltpu.VMEM((2, 2, slips + 1, pts, lane), F32),
            dma((3, 2)), dma((3, 2)), dma((2,)), dma((2,)),
            dma((2, max(chips_n - 1, 1))), dma((2, chips_n)), dma((2,)), dma((2,)),
        ],
        compiler_params=pltpu.CompilerParams(
            collective_id=0, has_side_effects=True, vmem_limit_bytes=56 * 1024 * 1024),
    )(adjacency, ops, schmid_map, hardening, history.reshape(vl * pts, local))
    return out.reshape(vl, pts, local)


def solution(mesh):
    in_specs = (P("var", None, "zone"), P(None, "zone"), P(), P(), P(), P())
    out_specs = P("var", None, "zone")
    return jax.shard_map(
        functools.partial(per_device, mesh.shape["zone"], mesh.shape["var"] // 2),
        mesh=mesh, in_specs=in_specs, out_specs=out_specs, check_vma=False
    )
```

```python
import functools

import jax
import jax.numpy as jnp
from jax import lax
from jax.experimental import pallas as pl
from jax.experimental.pallas import tpu as pltpu
from jax.sharding import PartitionSpec as P

F32 = jnp.float32
BF16 = jnp.bfloat16
MESH = pl.DeviceIdType.MESH
ROT = 4
TILE = 16


def split(x):
    hi = x.astype(BF16)
    return hi, (x - hi.astype(F32)).astype(BF16)


def kernel(sizes, adj_ref, op_ref, schmid_ref, hard_ref, h_ref, out_ref, one, two, cur, lcat, oh, hsend, hrecv, msg, mrecv, buf, tb,
           hs_sem, hr_sem, m_sem, mr_sem, x_sem, xr_sem, t_sem, tr_sem):
    zones_n, chips_n, vl, pts, local, faces, slips = sizes
    rim = local // 8
    lane = 2 * rim
    half = vl * pts // 2
    zone = lax.axis_index("zone")
    var = lax.axis_index("var")
    chip = var // 2
    core = var % 2
    mate = chip * 2 + (1 - core)
    has_left = zone > 0
    has_right = zone < zones_n - 1
    low = lax.broadcasted_iota(jnp.int32, (pts, lane), 1) < rim

    barrier = pltpu.get_barrier_semaphore()

    @pl.when(has_left)
    def _():
        pl.semaphore_signal(barrier, inc=1, device_id={"zone": zone - 1}, device_id_type=MESH)

    @pl.when(has_right)
    def _():
        pl.semaphore_signal(barrier, inc=1, device_id={"zone": zone + 1}, device_id_type=MESH)

    pl.semaphore_signal(barrier, inc=1, device_id={"var": mate}, device_id_type=MESH)
    for d in range(1, chips_n):
        peer = ((chip + d) % chips_n) * 2 + core
        pl.semaphore_signal(barrier, inc=1, device_id={"var": peer}, device_id_type=MESH)

    def halo_copy(s, side):
        target = zone + 1 if side == 0 else zone - 1
        return pltpu.make_async_remote_copy(
            src_ref=hsend.at[s, side], dst_ref=hrecv.at[s, side],
            send_sem=hs_sem.at[s, side], recv_sem=hr_sem.at[s, side],
            device_id={"zone": target}, device_id_type=MESH)

    def pack_edges(s, src):
        def body(i, _):
            top = pl.ds(pl.multiple_of(i * pts, pts), pts)
            bot = pl.ds(pl.multiple_of(half + i * pts, pts), pts)
            hsend[s, 0, top, :] = jnp.where(
                low, pltpu.roll(src[top, local - lane:local], rim, 1), src[bot, local - lane:local])
            hsend[s, 1, top, :] = jnp.where(
                low, src[top, 0:lane], pltpu.roll(src[bot, 0:lane], rim, 1))
            return 0
        lax.fori_loop(0, vl // 2, body, 0)

    def start_halo(s):
        @pl.when(has_right)
        def _():
            halo_copy(s, 0).start()

        @pl.when(has_left)
        def _():
            halo_copy(s, 1).start()

    def wait_halo(s):
        @pl.when(has_left)
        def _():
            halo_copy(s, 0).wait_recv()

        @pl.when(has_right)
        def _():
            halo_copy(s, 1).wait_recv()

    pack_edges(0, h_ref)

    @pl.when(jnp.logical_not(has_left))
    def _():
        for s in range(3):
            hrecv[s, 0] = jnp.zeros((half, lane), F32)

    @pl.when(jnp.logical_not(has_right))
    def _():
        for s in range(3):
            hrecv[s, 1] = jnp.zeros((half, lane), F32)

    pl.semaphore_wait(barrier, chips_n + has_left.astype(jnp.int32) + has_right.astype(jnp.int32))
    start_halo(0)

    op_hi, op_lo = split(op_ref[...])
    upper = lax.broadcasted_iota(jnp.int32, op_ref.shape, 0) < pts
    lcat[...] = jnp.where(upper, op_hi.astype(F32), op_lo.astype(F32)).astype(BF16)

    offset = zone * local
    k = lax.broadcasted_iota(jnp.int32, (2 * lane, lane), 0)
    for b in range(4):
        source = jnp.where(k < lane, lane * b + k,
                           jnp.where(k < lane + rim, lane * b + k, lane * (b - 2) + k))
        for f in range(faces):
            adj = adj_ref[f:f + 1, b * lane:(b + 1) * lane]
            adj = jnp.where(adj >= 0, adj - offset, -4 * local)
            oh[b, :, f * lane:(f + 1) * lane] = jnp.where(source == adj, 1.0, 0.0).astype(BF16)

    def v_rows(v):
        return pl.ds(pl.multiple_of(v * pts, pts), pts)

    def block(s, b, src, dst, halo=True):
        cols = slice(b * lane, (b + 1) * lane)

        def body(i, _):
            owns, terms = [], []
            for part in range(2):
                rows = v_rows(i + part * (vl // 2))
                own = src[rows, cols]
                if b > 0:
                    up = src[rows, (b - 1) * lane:b * lane]
                elif halo:
                    up = hrecv[s, 0, v_rows(i), :]
                    up = pltpu.roll(up, rim, 1) if part == 0 else up
                else:
                    up = jnp.zeros((pts, lane), F32)
                if b < 3:
                    down = src[rows, (b + 1) * lane:(b + 2) * lane]
                elif halo:
                    down = hrecv[s, 1, v_rows(i), :]
                    down = pltpu.roll(down, rim, 1) if part == 1 else down
                else:
                    down = jnp.zeros((pts, lane), F32)
                owns.append(own)
                terms.extend(split(jnp.concatenate([own, jnp.where(low, down, up)], axis=1)))
            g = jnp.dot(jnp.concatenate(terms, axis=0), oh[b],
                        preferred_element_type=F32).astype(BF16)
            rhs = []
            for part in range(2):
                pieces = []
                for t in range(2):
                    q = 2 * part + t
                    pieces += [g[q * pts:(q + 1) * pts, f * lane:(f + 1) * lane]
                               for f in range(faces)]
                    pieces.append(terms[q][:, 0:lane])
                rhs.append(jnp.concatenate(pieces, axis=0))
            r = jnp.dot(lcat[...], jnp.concatenate(rhs, axis=1), preferred_element_type=F32)
            r = r[0:pts] + r[pts:2 * pts]
            for part in range(2):
                rows = v_rows(i + part * (vl // 2))
                total = owns[part] + r[:, part * lane:(part + 1) * lane]
                if s == 1:
                    total = 0.75 * h_ref[rows, cols] + 0.25 * total
                elif s == 2:
                    total = h_ref[rows, cols] * (1.0 / 3.0) + (2.0 / 3.0) * total
                dst[rows, cols] = total
            return 0
        lax.fori_loop(0, vl // 2, body, 0, unroll=3 if vl % 6 == 0 else 1)

    def shear_chunk(col, dest, rot_row):
        def body(t, _):
            tr = pl.ds(pl.multiple_of(t * TILE, TILE), TILE)
            xs = [cur[pl.ds(pl.multiple_of(v * pts + t * TILE, TILE), TILE), pl.ds(col, lane)]
                  for v in range(vl)]
            for a in range(slips):
                y = xs[0] * schmid_ref[var * vl, a]
                for v in range(1, vl):
                    y = y + xs[v] * schmid_ref[var * vl + v, a]
                dest[a, tr, :] = y
            dest[rot_row, tr, :] = xs[0]
            return 0
        lax.fori_loop(0, pts // TILE, body, 0)

    def chunk_col(b, c):
        return pl.multiple_of((1 + c) * lane if b == 0 else 3 * c * lane, lane)

    def mate_copy(b):
        return pltpu.make_async_remote_copy(
            src_ref=msg.at[b], dst_ref=mrecv.at[b], send_sem=m_sem.at[b], recv_sem=mr_sem.at[b],
            device_id={"var": mate}, device_id_type=MESH)

    def chip_copy(b, d, slot):
        peer = ((chip + d) % chips_n) * 2 + core
        return pltpu.make_async_remote_copy(
            src_ref=buf.at[b, slot], dst_ref=buf.at[b, slot],
            send_sem=x_sem.at[b, d - 1], recv_sem=xr_sem.at[b, slot],
            device_id={"var": peer}, device_id_type=MESH)

    def tanh_copy(b, slot):
        return pltpu.make_async_remote_copy(
            src_ref=tb.at[b, slot], dst_ref=tb.at[b, slot],
            send_sem=t_sem.at[b], recv_sem=tr_sem.at[b],
            device_id={"var": mate}, device_id_type=MESH)

    def send_partial(b):
        shear_chunk(chunk_col(b, 1 - core), msg.at[b], slips)
        mate_copy(b).start()
        shear_chunk(chunk_col(b, core), buf.at[b, chip], slips + core)

    def send_chip(b):
        mate_copy(b).wait_recv()
        mine = buf.at[b, chip]
        for a in range(slips):
            mine[a] = mine[a] + mrecv[b, a]
        mine[slips + 1 - core] = mrecv[b, slips]
        for d in range(1, chips_n):
            chip_copy(b, d, chip).start()

    def renew(b):
        for d in range(1, chips_n):
            chip_copy(b, d, (chip + d) % chips_n).wait_recv()

        def body(t, _):
            tr = pl.ds(pl.multiple_of(t * TILE, TILE), TILE)
            ts = []
            for a in range(slips):
                y = buf[b, 0, a, tr, :]
                for c in range(1, chips_n):
                    y = y + buf[b, c, a, tr, :]
                ts.append(jnp.tanh(y))
                tb[b, core, a, tr, :] = ts[-1]
            total = None
            for k in range(ROT):
                y = buf[b, k // 2, slips + k % 2, tr, :]
                for a in range(slips):
                    y = y + ts[a] * hard_ref[a, k * vl]
                total = y * y if total is None else total + y * y
            tb[b, core, slips, tr, :] = 1.0 / jnp.maximum(jnp.sqrt(total), 1.0)
            return 0
        lax.fori_loop(0, pts // TILE, body, 0)
        tanh_copy(b, core).start()

    rotates = (jnp.full((TILE, lane), var, jnp.int32) < ROT)

    def write(b, c):
        col = chunk_col(b, c)

        def body(t, _):
            tr = pl.ds(pl.multiple_of(t * TILE, TILE), TILE)
            ts = [tb[b, c, a, tr, :] for a in range(slips)]
            for v in range(vl):
                rows = pl.ds(pl.multiple_of(v * pts + t * TILE, TILE), TILE)
                y = cur[rows, pl.ds(col, lane)]
                for a in range(slips):
                    y = y + ts[a] * hard_ref[a, var * vl + v]
                if v == 0:
                    y = jnp.where(rotates, y * tb[b, c, slips, tr, :], y)
                out_ref[rows, pl.ds(col, lane)] = y
            return 0
        lax.fori_loop(0, pts // TILE, body, 0)

    def both(s, blocks, src, dst, halo=True):
        for b in blocks:
            block(s, b, src, dst, halo)

    both(0, (1, 2), h_ref, one)
    wait_halo(0)
    both(0, (0, 3), h_ref, one)
    pack_edges(1, one)
    start_halo(1)
    both(1, (1, 2), one, two)
    both(1, (0, 3), one, two, halo=False)
    both(2, (1, 2), two, cur)
    send_partial(0)
    send_chip(0)
    wait_halo(1)
    both(1, (0, 3), one, two)
    pack_edges(2, two)
    start_halo(2)
    wait_halo(2)
    both(2, (0, 3), two, cur)
    send_partial(1)
    send_chip(1)
    for b in range(2):
        renew(b)
        write(b, core)
        tanh_copy(b, 1 - core).wait_recv()
        write(b, 1 - core)

    for s in range(3):
        @pl.when(has_right)
        def _():
            halo_copy(s, 0).wait_send()

        @pl.when(has_left)
        def _():
            halo_copy(s, 1).wait_send()
    for b in range(2):
        mate_copy(b).wait_send()
        tanh_copy(b, core).wait_send()
        for d in range(1, chips_n):
            chip_copy(b, d, chip).wait_send()


def per_device(zones_n, chips_n, history, adjacency, volume_op, face_lift, schmid_map, hardening):
    vl, pts, local = history.shape
    faces = face_lift.shape[0]
    slips = schmid_map.shape[1]
    lane, half = local // 4, vl * pts // 2
    ops = jnp.concatenate([face_lift, volume_op[None]], axis=0)
    ops = jnp.tile(ops.reshape((faces + 1) * pts, pts).T, (2, 2))
    vmem = pl.BlockSpec(memory_space=pltpu.VMEM)
    smem = pl.BlockSpec(memory_space=pltpu.SMEM)
    dma = pltpu.SemaphoreType.DMA
    out = pl.pallas_call(
        functools.partial(kernel, (zones_n, chips_n, vl, pts, local, faces, slips)),
        out_shape=jax.ShapeDtypeStruct((vl * pts, local), F32),
        in_specs=[vmem, vmem, smem, smem, vmem],
        out_specs=vmem,
        scratch_shapes=[
            pltpu.VMEM((vl * pts, local), F32),
            pltpu.VMEM((vl * pts, local), F32),
            pltpu.VMEM((vl * pts, local), F32),
            pltpu.VMEM((2 * pts, 2 * (faces + 1) * pts), BF16),
            pltpu.VMEM((4, 2 * lane, faces * lane), BF16),
            pltpu.VMEM((3, 2, half, lane), F32),
            pltpu.VMEM((3, 2, half, lane), F32),
            pltpu.VMEM((2, slips + 1, pts, lane), F32),
            pltpu.VMEM((2, slips + 1, pts, lane), F32),
            pltpu.VMEM((2, chips_n, slips + 2, pts, lane), F32),
            pltpu.VMEM((2, 2, slips + 1, pts, lane), F32),
            dma((3, 2)), dma((3, 2)), dma((2,)), dma((2,)),
            dma((2, max(chips_n - 1, 1))), dma((2, chips_n)), dma((2,)), dma((2,)),
        ],
        compiler_params=pltpu.CompilerParams(
            collective_id=0, has_side_effects=True, vmem_limit_bytes=56 * 1024 * 1024),
    )(adjacency, ops, schmid_map, hardening, history.reshape(vl * pts, local))
    return out.reshape(vl, pts, local)


def solution(mesh):
    in_specs = (P("var", None, "zone"), P(None, "zone"), P(), P(), P(), P())
    out_specs = P("var", None, "zone")
    return jax.shard_map(
        functools.partial(per_device, mesh.shape["zone"], mesh.shape["var"] // 2),
        mesh=mesh, in_specs=in_specs, out_specs=out_specs, check_vma=False
    )
```

```python
import functools

import jax
import jax.numpy as jnp
from jax import lax
from jax.experimental import pallas as pl
from jax.experimental.pallas import tpu as pltpu
from jax.sharding import PartitionSpec as P

F32 = jnp.float32
BF16 = jnp.bfloat16
MESH = pl.DeviceIdType.MESH
ROT = 4
TILE = 16


def split(x):
    hi = x.astype(BF16)
    return hi, (x - hi.astype(F32)).astype(BF16)


def kernel(sizes, adj_ref, op_ref, schmid_ref, hard_ref, h_ref, out_ref, one, two, cur, lcat, oh, hsend, hrecv, msg, mrecv, buf, tb,
           hs_sem, hr_sem, m_sem, mr_sem, x_sem, xr_sem, t_sem, tr_sem):
    zones_n, chips_n, vl, pts, local, faces, slips = sizes
    rim = local // 8
    lane = 2 * rim
    half = vl * pts // 2
    zone = lax.axis_index("zone")
    var = lax.axis_index("var")
    chip = var // 2
    core = var % 2
    mate = chip * 2 + (1 - core)
    has_left = zone > 0
    has_right = zone < zones_n - 1
    low = lax.broadcasted_iota(jnp.int32, (pts, lane), 1) < rim

    barrier = pltpu.get_barrier_semaphore()

    @pl.when(has_left)
    def _():
        pl.semaphore_signal(barrier, inc=1, device_id={"zone": zone - 1}, device_id_type=MESH)

    @pl.when(has_right)
    def _():
        pl.semaphore_signal(barrier, inc=1, device_id={"zone": zone + 1}, device_id_type=MESH)

    pl.semaphore_signal(barrier, inc=1, device_id={"var": mate}, device_id_type=MESH)
    for d in range(1, chips_n):
        peer = ((chip + d) % chips_n) * 2 + core
        pl.semaphore_signal(barrier, inc=1, device_id={"var": peer}, device_id_type=MESH)

    def halo_copy(s, side):
        target = zone + 1 if side == 0 else zone - 1
        return pltpu.make_async_remote_copy(
            src_ref=hsend.at[s, side], dst_ref=hrecv.at[s, side],
            send_sem=hs_sem.at[s, side], recv_sem=hr_sem.at[s, side],
            device_id={"zone": target}, device_id_type=MESH)

    def pack_edges(s, src):
        def body(i, _):
            top = pl.ds(pl.multiple_of(i * pts, pts), pts)
            bot = pl.ds(pl.multiple_of(half + i * pts, pts), pts)
            hsend[s, 0, top, :] = jnp.where(
                low, pltpu.roll(src[top, local - lane:local], rim, 1), src[bot, local - lane:local])
            hsend[s, 1, top, :] = jnp.where(
                low, src[top, 0:lane], pltpu.roll(src[bot, 0:lane], rim, 1))
            return 0
        lax.fori_loop(0, vl // 2, body, 0)

    def start_halo(s):
        @pl.when(has_right)
        def _():
            halo_copy(s, 0).start()

        @pl.when(has_left)
        def _():
            halo_copy(s, 1).start()

    def wait_halo(s):
        @pl.when(has_left)
        def _():
            halo_copy(s, 0).wait_recv()

        @pl.when(has_right)
        def _():
            halo_copy(s, 1).wait_recv()

    pack_edges(0, h_ref)

    @pl.when(jnp.logical_not(has_left))
    def _():
        for s in range(3):
            hrecv[s, 0] = jnp.zeros((half, lane), F32)

    @pl.when(jnp.logical_not(has_right))
    def _():
        for s in range(3):
            hrecv[s, 1] = jnp.zeros((half, lane), F32)

    pl.semaphore_wait(barrier, chips_n + has_left.astype(jnp.int32) + has_right.astype(jnp.int32))
    start_halo(0)

    op_hi, op_lo = split(op_ref[...])
    upper = lax.broadcasted_iota(jnp.int32, op_ref.shape, 0) < pts
    lcat[...] = jnp.where(upper, op_hi.astype(F32), op_lo.astype(F32)).astype(BF16)

    offset = zone * local
    k = lax.broadcasted_iota(jnp.int32, (2 * lane, lane), 0)
    for b in range(4):
        source = jnp.where(k < lane, lane * b + k,
                           jnp.where(k < lane + rim, lane * b + k, lane * (b - 2) + k))
        for f in range(faces):
            adj = adj_ref[f:f + 1, b * lane:(b + 1) * lane]
            adj = jnp.where(adj >= 0, adj - offset, -4 * local)
            oh[b, :, f * lane:(f + 1) * lane] = jnp.where(source == adj, 1.0, 0.0).astype(BF16)

    def v_rows(v):
        return pl.ds(pl.multiple_of(v * pts, pts), pts)

    def block(s, b, src, dst, halo=True):
        cols = slice(b * lane, (b + 1) * lane)

        def body(i, _):
            owns, terms = [], []
            for part in range(2):
                rows = v_rows(i + part * (vl // 2))
                own = src[rows, cols]
                if b > 0:
                    up = src[rows, (b - 1) * lane:b * lane]
                elif halo:
                    up = hrecv[s, 0, v_rows(i), :]
                    up = pltpu.roll(up, rim, 1) if part == 0 else up
                else:
                    up = jnp.zeros((pts, lane), F32)
                if b < 3:
                    down = src[rows, (b + 1) * lane:(b + 2) * lane]
                elif halo:
                    down = hrecv[s, 1, v_rows(i), :]
                    down = pltpu.roll(down, rim, 1) if part == 1 else down
                else:
                    down = jnp.zeros((pts, lane), F32)
                owns.append(own)
                terms.extend(split(jnp.concatenate([own, jnp.where(low, down, up)], axis=1)))
            g = jnp.dot(jnp.concatenate(terms, axis=0), oh[b],
                        preferred_element_type=F32).astype(BF16)
            rhs = []
            for part in range(2):
                pieces = []
                for t in range(2):
                    q = 2 * part + t
                    pieces += [g[q * pts:(q + 1) * pts, f * lane:(f + 1) * lane]
                               for f in range(faces)]
                    pieces.append(terms[q][:, 0:lane])
                rhs.append(jnp.concatenate(pieces, axis=0))
            r = jnp.dot(lcat[...], jnp.concatenate(rhs, axis=1), preferred_element_type=F32)
            r = r[0:pts] + r[pts:2 * pts]
            for part in range(2):
                rows = v_rows(i + part * (vl // 2))
                total = owns[part] + r[:, part * lane:(part + 1) * lane]
                if s == 1:
                    total = 0.75 * h_ref[rows, cols] + 0.25 * total
                elif s == 2:
                    total = h_ref[rows, cols] * (1.0 / 3.0) + (2.0 / 3.0) * total
                dst[rows, cols] = total
            return 0
        lax.fori_loop(0, vl // 2, body, 0, unroll=vl // 2)

    def shear_chunk(col, dest, rot_row):
        def body(t, _):
            tr = pl.ds(pl.multiple_of(t * TILE, TILE), TILE)
            xs = [cur[pl.ds(pl.multiple_of(v * pts + t * TILE, TILE), TILE), pl.ds(col, lane)]
                  for v in range(vl)]
            for a in range(slips):
                y = xs[0] * schmid_ref[var * vl, a]
                for v in range(1, vl):
                    y = y + xs[v] * schmid_ref[var * vl + v, a]
                dest[a, tr, :] = y
            dest[rot_row, tr, :] = xs[0]
            return 0
        lax.fori_loop(0, pts // TILE, body, 0)

    def chunk_col(b, c):
        return pl.multiple_of((1 + c) * lane if b == 0 else 3 * c * lane, lane)

    def mate_copy(b):
        return pltpu.make_async_remote_copy(
            src_ref=msg.at[b], dst_ref=mrecv.at[b], send_sem=m_sem.at[b], recv_sem=mr_sem.at[b],
            device_id={"var": mate}, device_id_type=MESH)

    def chip_copy(b, d, slot):
        peer = ((chip + d) % chips_n) * 2 + core
        return pltpu.make_async_remote_copy(
            src_ref=buf.at[b, slot], dst_ref=buf.at[b, slot],
            send_sem=x_sem.at[b, d - 1], recv_sem=xr_sem.at[b, slot],
            device_id={"var": peer}, device_id_type=MESH)

    def tanh_copy(b, slot):
        return pltpu.make_async_remote_copy(
            src_ref=tb.at[b, slot], dst_ref=tb.at[b, slot],
            send_sem=t_sem.at[b], recv_sem=tr_sem.at[b],
            device_id={"var": mate}, device_id_type=MESH)

    def send_partial(b):
        shear_chunk(chunk_col(b, 1 - core), msg.at[b], slips)
        mate_copy(b).start()
        shear_chunk(chunk_col(b, core), buf.at[b, chip], slips + core)

    def send_chip(b):
        mate_copy(b).wait_recv()
        mine = buf.at[b, chip]
        for a in range(slips):
            mine[a] = mine[a] + mrecv[b, a]
        mine[slips + 1 - core] = mrecv[b, slips]
        for d in range(1, chips_n):
            chip_copy(b, d, chip).start()

    def renew(b):
        for d in range(1, chips_n):
            chip_copy(b, d, (chip + d) % chips_n).wait_recv()

        def body(t, _):
            tr = pl.ds(pl.multiple_of(t * TILE, TILE), TILE)
            ts = []
            for a in range(slips):
                y = buf[b, 0, a, tr, :]
                for c in range(1, chips_n):
                    y = y + buf[b, c, a, tr, :]
                ts.append(jnp.tanh(y))
                tb[b, core, a, tr, :] = ts[-1]
            total = None
            for k in range(ROT):
                y = buf[b, k // 2, slips + k % 2, tr, :]
                for a in range(slips):
                    y = y + ts[a] * hard_ref[a, k * vl]
                total = y * y if total is None else total + y * y
            tb[b, core, slips, tr, :] = 1.0 / jnp.maximum(jnp.sqrt(total), 1.0)
            return 0
        lax.fori_loop(0, pts // TILE, body, 0)
        tanh_copy(b, core).start()

    rotates = (jnp.full((TILE, lane), var, jnp.int32) < ROT)

    def write(b, c):
        col = chunk_col(b, c)

        def body(t, _):
            tr = pl.ds(pl.multiple_of(t * TILE, TILE), TILE)
            ts = [tb[b, c, a, tr, :] for a in range(slips)]
            for v in range(vl):
                rows = pl.ds(pl.multiple_of(v * pts + t * TILE, TILE), TILE)
                y = cur[rows, pl.ds(col, lane)]
                for a in range(slips):
                    y = y + ts[a] * hard_ref[a, var * vl + v]
                if v == 0:
                    y = jnp.where(rotates, y * tb[b, c, slips, tr, :], y)
                out_ref[rows, pl.ds(col, lane)] = y
            return 0
        lax.fori_loop(0, pts // TILE, body, 0)

    def both(s, blocks, src, dst, halo=True):
        for b in blocks:
            block(s, b, src, dst, halo)

    both(0, (1, 2), h_ref, one)
    wait_halo(0)
    both(0, (0, 3), h_ref, one)
    pack_edges(1, one)
    start_halo(1)
    both(1, (1, 2), one, two)
    both(1, (0, 3), one, two, halo=False)
    both(2, (1, 2), two, cur)
    send_partial(0)
    send_chip(0)
    wait_halo(1)
    both(1, (0, 3), one, two)
    pack_edges(2, two)
    start_halo(2)
    wait_halo(2)
    both(2, (0, 3), two, cur)
    send_partial(1)
    send_chip(1)
    for b in range(2):
        renew(b)
        write(b, core)
        tanh_copy(b, 1 - core).wait_recv()
        write(b, 1 - core)

    for s in range(3):
        @pl.when(has_right)
        def _():
            halo_copy(s, 0).wait_send()

        @pl.when(has_left)
        def _():
            halo_copy(s, 1).wait_send()
    for b in range(2):
        mate_copy(b).wait_send()
        tanh_copy(b, core).wait_send()
        for d in range(1, chips_n):
            chip_copy(b, d, chip).wait_send()


def per_device(zones_n, chips_n, history, adjacency, volume_op, face_lift, schmid_map, hardening):
    vl, pts, local = history.shape
    faces = face_lift.shape[0]
    slips = schmid_map.shape[1]
    lane, half = local // 4, vl * pts // 2
    ops = jnp.concatenate([face_lift, volume_op[None]], axis=0)
    ops = jnp.tile(ops.reshape((faces + 1) * pts, pts).T, (2, 2))
    vmem = pl.BlockSpec(memory_space=pltpu.VMEM)
    smem = pl.BlockSpec(memory_space=pltpu.SMEM)
    dma = pltpu.SemaphoreType.DMA
    out = pl.pallas_call(
        functools.partial(kernel, (zones_n, chips_n, vl, pts, local, faces, slips)),
        out_shape=jax.ShapeDtypeStruct((vl * pts, local), F32),
        in_specs=[vmem, vmem, smem, smem, vmem],
        out_specs=vmem,
        scratch_shapes=[
            pltpu.VMEM((vl * pts, local), F32),
            pltpu.VMEM((vl * pts, local), F32),
            pltpu.VMEM((vl * pts, local), F32),
            pltpu.VMEM((2 * pts, 2 * (faces + 1) * pts), BF16),
            pltpu.VMEM((4, 2 * lane, faces * lane), BF16),
            pltpu.VMEM((3, 2, half, lane), F32),
            pltpu.VMEM((3, 2, half, lane), F32),
            pltpu.VMEM((2, slips + 1, pts, lane), F32),
            pltpu.VMEM((2, slips + 1, pts, lane), F32),
            pltpu.VMEM((2, chips_n, slips + 2, pts, lane), F32),
            pltpu.VMEM((2, 2, slips + 1, pts, lane), F32),
            dma((3, 2)), dma((3, 2)), dma((2,)), dma((2,)),
            dma((2, max(chips_n - 1, 1))), dma((2, chips_n)), dma((2,)), dma((2,)),
        ],
        compiler_params=pltpu.CompilerParams(
            collective_id=0, has_side_effects=True, vmem_limit_bytes=56 * 1024 * 1024),
    )(adjacency, ops, schmid_map, hardening, history.reshape(vl * pts, local))
    return out.reshape(vl, pts, local)


def solution(mesh):
    in_specs = (P("var", None, "zone"), P(None, "zone"), P(), P(), P(), P())
    out_specs = P("var", None, "zone")
    return jax.shard_map(
        functools.partial(per_device, mesh.shape["zone"], mesh.shape["var"] // 2),
        mesh=mesh, in_specs=in_specs, out_specs=out_specs, check_vma=False
    )
```
